32 devices in a mesh: rep: 2 (over y), tp: 16 (over z, x, core).
Axes of the slice: x: 2, y: 2, z: 4, core: 2. Of those that a mesh axis runs over, the one named last changes fastest.
Arguments:
- queries: bfloat16 [4096, 16384], P(('rep', 'tp')), parts along dimension 0, may hold values from -120 to 120
- keyvals: bfloat16 [4096, 2048], P(('rep', 'tp')), parts along dimension 0, may hold values from -6 to 6
- parent: int32 [32], P('rep'), parts along dimension 0, may hold values from -1 to 13, as said below
- counts: int32 [32], P('rep'), parts along dimension 0, may hold values from 32 to 128
Outputs:
- attended: bfloat16 [4096, 16384], P(('rep', 'tp')), parts along dimension 0
The draws below stay inside these ranges and needn't reach their ends.
There are 2 independent parts, one for each index of `rep`. The reference program is written for one: setup_inputs(seed, part) draws one part's arguments, and reference() takes and returns one part's arrays. A program takes and returns all parts, laid end to end along the dimension named above; each array names one. Nothing has to cross between parts.
Inputs may be any that keep to these rules, and one draw needn't show every extreme that they name: Segments whose numbers agree modulo 16 // 8 form one tree of 8 segments; the lowest of a tree has parent -1, every other one a parent with a lower number in its tree. In every draw some segment has 7 ancestors.
All inputs are finite; a program needn't handle non-finite values.
Results may differ from the reference program's by a relative error of at most 0.004.
Values may be sent and summed in bfloat16 or wider, within the bound.
No kernel may reach another device: no remote copies, remote signals or barrier semaphores. Data moves between devices by JAX's collectives and lax.ppermute only.
A program may use at most 128 MiB of HBM per device.

```python
import jax
import jax.numpy as jnp
from jax import lax

HEADS = 128
HD = 128
KVH = 8
GROUP = 16
SEG = 128
SPAN = 8
NSEG = 16
TOKENS = 2048


def shared_keys(key):
    return jax.random.normal(key, (TOKENS, KVH, HD), jnp.float32)


def draw_keyvals(key, part):
    keys = shared_keys(key)
    key = jax.random.fold_in(key, 11)
    values = jax.random.normal(jax.random.fold_in(key, 1), (TOKENS, KVH, HD), jnp.float32)
    keys = jnp.clip(keys, -6.0, 6.0)
    values = jnp.clip(values, -6.0, 6.0)
    return jnp.stack([keys, values], axis=2).reshape(TOKENS, KVH * 2 * HD).astype(jnp.bfloat16)


def draw_queries(key, part):
    key = jax.random.fold_in(key, 23)
    result = jnp.clip(jax.random.normal(key, (TOKENS, KVH, GROUP, HD), jnp.float32), -6.0, 6.0)
    return result.reshape(TOKENS, KVH * GROUP * HD).astype(jnp.bfloat16)


def draw_parent(key, part):
    key = jax.random.fold_in(key, 37)
    stride = NSEG // SPAN
    segment_ids = jnp.arange(NSEG, dtype=jnp.int32)
    tree = segment_ids % stride
    offset = segment_ids // stride
    picks = jax.random.randint(key, (NSEG,), 0, 1 << 20)
    chosen = tree + stride * (picks % jnp.maximum(offset, 1))
    chain_tree = jax.random.randint(jax.random.fold_in(key, 1), (), 0, stride)
    chosen = jnp.where(tree == chain_tree, segment_ids - stride, chosen)
    return jnp.where(offset == 0, -1, chosen).astype(jnp.int32)


def touch_ends(values, own_key, smallest, top_value):
    longest = values.shape.index(max(values.shape))
    spots = []
    for shift in (0, 1):
        where = [jax.random.randint(jax.random.fold_in(own_key, axis), (), 0, length) for axis, length in enumerate(values.shape)]
        where[longest] = (where[longest] + shift) % values.shape[longest]
        spots.append(tuple(where))
    return values.at[spots[0]].set(smallest).at[spots[1]].set(top_value)


def setup_inputs(seed: int = 0, part: int = 0) -> dict:
    seeds = jax.random.split(jax.random.key(seed), 5)
    part_keys = jax.random.split(jax.random.fold_in(seeds[4], part), 5)
    return {
        "queries": draw_queries(jax.random.fold_in(jax.random.fold_in(seeds[4], part), 71), part),
        "keyvals": draw_keyvals(jax.random.fold_in(jax.random.fold_in(seeds[4], part), 71), part),
        "parent": draw_parent(jax.random.fold_in(jax.random.fold_in(seeds[4], part), 71), part),
        "counts": touch_ends(jax.random.randint(part_keys[3], (NSEG,), SEG // 4, SEG + 1), jax.random.fold_in(part_keys[3], 1), SEG // 4, SEG).astype(jnp.int32),
    }


def lookup(table, index):
    entries = jnp.arange(table.shape[0], dtype=jnp.int32)
    hit = index[:, None] == entries[None, :]
    found = jnp.sum(jnp.where(hit, table[None, :], 0), axis=1).astype(jnp.int32)
    return jnp.where(index >= 0, found, -1).astype(jnp.int32)


def ancestor_table(parent, levels):
    current = jnp.arange(parent.shape[0], dtype=jnp.int32)
    columns = [current]
    for level in range(1, levels):
        current = lookup(parent, current)
        columns.append(current)
    return jnp.stack(columns, axis=1)


def reference(queries, keyvals, parent, counts):
    scale = HD ** -0.5
    chains = ancestor_table(parent, SPAN)
    query_blocks = queries.reshape(NSEG, SEG, KVH, GROUP, HD)
    kv_blocks = keyvals.reshape(NSEG, SEG, KVH, 2, HD)
    position = jnp.arange(SEG, dtype=jnp.int32)
    level_ids = jnp.arange(SPAN, dtype=jnp.int32)

    def one_segment(segment):
        owners = chains[segment]
        present = owners >= 0
        source = jnp.maximum(owners, 0).astype(jnp.int32)
        gathered = kv_blocks[source]
        keys = gathered[:, :, :, 0].astype(jnp.float32)
        values = gathered[:, :, :, 1].astype(jnp.float32)
        lengths = counts[source]
        valid = present[:, None] & (position[None, :] < lengths[:, None])
        ordered = (level_ids[None, :, None] > 0) | (position[None, None, :] <= position[:, None, None])
        allowed = valid[None, :, :] & ordered
        local = query_blocks[segment].astype(jnp.float32)
        scores = jnp.einsum("ikgd,ljkd->kgilj", local, keys) * scale
        scores = jnp.where(allowed[None, None], scores, -1e30)
        top = jnp.max(scores, axis=(3, 4), keepdims=True)
        weights = jnp.exp(scores - top)
        total = jnp.sum(weights, axis=(3, 4))
        rounded = lax.optimization_barrier(weights.astype(jnp.bfloat16)).astype(jnp.float32)
        mixed = jnp.einsum("kgilj,ljkd->kgid", rounded, values)
        result = mixed / total[..., None]
        live = position < counts[segment]
        result = jnp.where(live[None, None, :, None], result, 0.0)
        return jnp.transpose(result, (2, 0, 1, 3)).reshape(SEG, HEADS * HD).astype(jnp.bfloat16)

    outputs = lax.map(one_segment, jnp.arange(NSEG, dtype=jnp.int32))
    return outputs.reshape(TOKENS, HEADS * HD)
```

```python
from functools import partial

import jax
import jax.numpy as jnp
from jax import lax
from jax.experimental import pallas as pl
from jax.experimental.pallas import tpu as pltpu
from jax.sharding import PartitionSpec as P

HD = 128
SPAN = 8
TILE = 32
NEG = -1e30
SCALE = HD ** (-0.5)
FACTOR = SCALE * 1.4426950408889634
LIMIT = (64.0 / SCALE) ** 2 / 1.02
STATE = HD + 8
VROWS = HD + 16
TOTAL, SHIFT, QNORM = HD, HD + 1, HD + 2


def is_ancestor(parent_ref, me, source):
    current = me
    hit = jnp.int32(0)
    for _ in range(SPAN - 1):
        current = jnp.where(current >= 0, parent_ref[jnp.maximum(current, 0)], -1)
        hit = jnp.where(current == source, 1, hit)
    return jnp.where(source >= 0, hit, 0)


def source_of(me, stride, shift, swap):
    offset = me // stride
    base = offset
    if swap:
        base = jnp.where(offset % 2 == 0, offset + 1, offset - 1)
    base = base - shift
    return jnp.where(base >= 0, base * stride + me % stride, -1)


def live_keys(parent_ref, counts_ref, me, stride, move):
    if move is None:
        return counts_ref[me]
    source = source_of(me, stride, *move)
    length = counts_ref[jnp.maximum(source, 0)]
    return jnp.where(is_ancestor(parent_ref, me, source) > 0, length, 0)


def attend(stride, moves, first, last, aliased, me_ref, parent_ref, counts_ref, *refs):
    refs = list(refs)
    n = len(moves)
    if first:
        q_ref = refs.pop(0)
    else:
        qt_ref, old_ref = refs[:2]
        refs = refs[2:]
    kv_refs = refs[:n]
    refs = refs[n + (1 if aliased else 0):]
    if last:
        out_ref = refs.pop(0)
    else:
        if first:
            qt_ref = refs.pop(0)
        new_ref = refs.pop(0)
    k_buf, v_buf, top_buf = refs

    me = me_ref[0]
    count = counts_ref[me]
    rows = kv_refs[0].shape[0]
    tiles_max = rows // TILE
    lanes = (new_ref if not last else old_ref).shape[3]
    group = lanes // TILE
    tiles = (count + TILE - 1) // TILE
    lengths = [live_keys(parent_ref, counts_ref, me, stride, m) for m in moves]

    j_rows = lax.broadcasted_iota(jnp.int32, (rows, HD), 0)
    j_lanes = lax.broadcasted_iota(jnp.int32, (VROWS - HD, rows), 1)
    sub = lax.broadcasted_iota(jnp.int32, (VROWS - HD, rows), 0)
    ones = jnp.ones((HD, HD), jnp.bfloat16)
    key_norm = None
    for l in range(n):
        part = slice(l * rows, (l + 1) * rows)
        key = kv_refs[l][:, :HD]
        k_buf[part, :] = key
        value = jnp.where(j_rows < lengths[l], kv_refs[l][:, HD:].astype(jnp.float32), 0.0)
        v_buf[:HD, part] = value.astype(jnp.bfloat16).T
        live = (j_lanes < lengths[l]) & (sub == 0)
        v_buf[HD:, part] = jnp.where(live, 1.0, 0.0).astype(jnp.bfloat16)
        square = (key.astype(jnp.float32) * key.astype(jnp.float32)).astype(jnp.bfloat16)
        norm = jnp.max(jnp.dot(square, ones, preferred_element_type=jnp.float32), axis=0, keepdims=True)
        key_norm = norm if key_norm is None else jnp.maximum(key_norm, norm)
    key_norm = jnp.max(key_norm)

    def span(t):
        if isinstance(t, int):
            return slice(t * TILE, (t + 1) * TILE)
        return pl.ds(pl.multiple_of(t * TILE, TILE), TILE)

    if first:
        def turn(t, _):
            heads = [q_ref[span(t), g * HD:(g + 1) * HD] for g in range(group)]
            q = jnp.concatenate(heads, axis=0).T
            qt_ref[0, t] = q
            wide = q.astype(jnp.float32)
            top_buf[pl.ds(t, 1), :] = jnp.sum(wide * wide, axis=0, keepdims=True)
            return 0

        top_buf[...] = jnp.zeros(top_buf.shape, jnp.float32)
        lax.fori_loop(0, tiles, turn, 0)
        safe = jnp.max(top_buf[...]) * key_norm <= LIMIT
    else:
        top_buf[...] = jnp.zeros(top_buf.shape, jnp.float32)

        def check(t, _):
            bound = old_ref[0, t, QNORM:QNORM + 1, :] * key_norm
            moved = old_ref[0, t, SHIFT:SHIFT + 1, :] != 0.0
            top_buf[pl.ds(t, 1), :] = jnp.where(moved, 2.0 * LIMIT, bound)
            return 0

        lax.fori_loop(0, tiles, check, 0)
        safe = jnp.max(top_buf[...]) <= LIMIT

    def causal(t):
        j = lax.broadcasted_iota(jnp.int32, (rows, lanes), 0)
        i = lax.broadcasted_iota(jnp.int32, (rows, lanes), 1) % TILE + t * TILE
        return j <= i

    def scores(t):
        return jnp.dot(k_buf[...], qt_ref[0, t], preferred_element_type=jnp.float32)

    def finish(t, mixed, shift):
        if last:
            result = (mixed[:HD] * (1.0 / mixed[TOTAL:TOTAL + 1])).T
            base = t * TILE
            live = lax.broadcasted_iota(jnp.int32, (TILE, HD), 0) + base < count
            for g in range(group):
                piece = jnp.where(live, result[g * TILE:(g + 1) * TILE], 0.0)
                out_ref[span(t), g * HD:(g + 1) * HD] = piece.astype(out_ref.dtype)
        else:
            new_ref[0, t] = mixed[:STATE]
            new_ref[0, t, SHIFT:SHIFT + 1, :] = shift
            if first:
                new_ref[0, t, QNORM:QNORM + 1, :] = top_buf[pl.ds(t, 1), :]
            else:
                new_ref[0, t, QNORM:QNORM + 1, :] = old_ref[0, t, QNORM:QNORM + 1, :]

    def mix(weights):
        return jnp.dot(v_buf[...], weights, preferred_element_type=jnp.float32)

    def unshifted(t, s):
        w = jnp.exp2(s * FACTOR)
        if first:
            own = jnp.where(causal(t), w[:rows], 0.0)
            w = jnp.concatenate([own, w[rows:]], axis=0) if n > 1 else own
        mixed = mix(w.astype(jnp.bfloat16))[:STATE]
        if not first:
            mixed = mixed + old_ref[0, t]
        finish(t, mixed, jnp.zeros((1, lanes), jnp.float32))

    def shifted(t, _):
        s = scores(t)
        parts = []
        for l in range(n):
            j = lax.broadcasted_iota(jnp.int32, (rows, lanes), 0)
            allowed = j < lengths[l]
            if moves[l] is None:
                allowed = allowed & causal(t)
            parts.append(jnp.where(allowed, s[l * rows:(l + 1) * rows], NEG))
        s = jnp.concatenate(parts, axis=0)
        top = jnp.max(s, axis=0, keepdims=True)
        if not first:
            before = old_ref[0, t, SHIFT:SHIFT + 1, :]
            top = jnp.maximum(top, before)
        w = jnp.exp2((s - top) * FACTOR)
        mixed = mix(w.astype(jnp.bfloat16))[:STATE]
        if not first:
            mixed = mixed + old_ref[0, t] * jnp.exp2((before - top) * FACTOR)
        finish(t, mixed, top)
        return 0

    def run(k):
        s = scores(0)
        for t in range(k):
            following = scores(t + 1) if t + 1 < k else None
            unshifted(t, s)
            s = following

    for k in range(1, tiles_max + 1):
        pl.when(safe & (tiles == k))(partial(run, k))

    @pl.when(jnp.logical_not(safe))
    def _():
        lax.fori_loop(0, tiles, shifted, 0)

    if last:
        def clear(t, _):
            out_ref[span(t), :] = jnp.zeros((TILE, out_ref.shape[1]), out_ref.dtype)
            return 0

        lax.fori_loop(tiles, tiles_max, clear, 0)


def levels(stride, scalars, queries, kv_heads, moves, kvs, state, part, into=None, last=False):
    rows, width = queries.shape
    group = width // HD // kv_heads
    half = kv_heads // 2
    tiles_max = rows // TILE
    lanes = group * TILE
    turned = pl.BlockSpec((1, tiles_max, HD, lanes), lambda k, *_: (k, 0, 0, 0))
    held = pl.BlockSpec((1, tiles_max, STATE, lanes), lambda k, *_: (k, 0, 0, 0))
    first = state is None
    wide = pl.BlockSpec((rows, group * HD), lambda k, *_: (0, k + part * half))
    specs = [wide] if first else [turned, held]
    operands = [queries] if first else list(state)
    for array, offset in kvs:
        specs.append(pl.BlockSpec((rows, 2 * HD), lambda k, *_, offset=offset: (0, k + offset)))
        operands.append(array)
    aliases = {}
    if into is not None:
        specs.append(pl.BlockSpec(memory_space=pl.ANY))
        aliases = {3 + len(operands): 0}
        operands.append(into)
    if last:
        out_specs, out_shape = wide, jax.ShapeDtypeStruct((rows, width), jnp.bfloat16)
    else:
        out_specs = [turned, held]
        out_shape = [
            jax.ShapeDtypeStruct((half, tiles_max, HD, lanes), jnp.bfloat16),
            jax.ShapeDtypeStruct((half, tiles_max, STATE, lanes), jnp.float32),
        ]
        if not first:
            out_specs, out_shape = out_specs[1:], out_shape[1:]
    n = len(moves)
    return pl.pallas_call(
        partial(attend, stride, moves, first, last, into is not None),
        grid_spec=pltpu.PrefetchScalarGridSpec(
            num_scalar_prefetch=3,
            grid=(half,),
            in_specs=specs,
            out_specs=out_specs,
            scratch_shapes=[
                pltpu.VMEM((n * rows, HD), jnp.bfloat16),
                pltpu.VMEM((VROWS, n * rows), jnp.bfloat16),
                pltpu.VMEM((max(8, tiles_max), lanes), jnp.float32),
            ],
        ),
        out_shape=out_shape,
        input_output_aliases=aliases,
        compiler_params=pltpu.CompilerParams(vmem_limit_bytes=24 * 1024 * 1024),
        cost_estimate=pl.CostEstimate(
            flops=2 * rows * rows * width * n,
            bytes_accessed=4 * rows * width,
            transcendentals=rows * rows * width // HD * n // 2,
        ),
        name="last_levels" if last else "first_levels",
    )(*scalars, *operands)


def per_device(queries, keyvals, parent, counts):
    rows, width = queries.shape
    kv_heads = keyvals.shape[1] // (2 * HD)
    half = kv_heads // 2
    segments = lax.axis_size("tp")
    stride = segments // SPAN
    me = lax.axis_index("tp").reshape(1).astype(jnp.int32)

    def send(x, pairs):
        full = [(a * stride + t, b * stride + t) for a, b in pairs for t in range(stride)]
        return lax.ppermute(x, "tp", full)

    kernel = partial(levels, stride, (me, parent, counts), queries, kv_heads)

    swap = [(o, o ^ 1) for o in range(SPAN)]
    up = [[(o, o + 2) for o in range(low, SPAN - 2)] for low in (0, 2, 4)]
    cut = half * 2 * HD
    hold = lax.optimization_barrier
    a, b = keyvals[:, :cut], keyvals[:, cut:]
    az1, ax1 = send(a, up[0]), send(a, swap)
    bz1, bx1 = send(b, up[0]), send(b, swap)
    az1, ax1 = hold((az1, ax1))
    az2, ax2 = send(az1, up[1]), send(az1, swap)
    bz1, bx1 = hold((bz1, bx1))
    bz2, bx2 = send(bz1, up[1]), send(bz1, swap)
    az2, ax2 = hold((az2, ax2))
    az3, ax3 = send(az2, up[2]), send(az2, swap)
    bz2, bx2 = hold((bz2, bx2))
    bz3, bx3 = send(bz2, up[2]), send(bz2, swap)
    az3, ax3 = hold((az3, ax3))
    a4 = send(az3, swap)
    bz3, bx3 = hold((bz3, bx3))
    b4 = send(bx3, up[2])

    early = [None, (2, False), (0, True), (4, False), (2, True)]
    late = [(6, False), (4, True), (6, True)]
    state_a = kernel(early, [(keyvals, 0), (az1, 0), (ax1, 0), (az2, 0), (ax2, 0)], None, 0)
    state_b = kernel(early, [(keyvals, half), (bz1, 0), (bx1, 0), (bz2, 0), (bx2, 0)], None, 1)
    out = kernel(late, [(az3, 0), (ax3, 0), (a4, 0)], state_a, 0, last=True)
    return kernel(late, [(bz3, 0), (bx3, 0), (b4, 0)], state_b, 1, into=out, last=True)


def solution(mesh):
    in_specs = (P(("rep", "tp"), None), P(("rep", "tp"), None), P("rep"), P("rep"))
    out_specs = P(("rep", "tp"), None)
    return jax.shard_map(
        per_device, mesh=mesh, in_specs=in_specs, out_specs=out_specs, check_vma=False
    )
```

```python
from functools import partial

import jax
import jax.numpy as jnp
from jax import lax
from jax.experimental import pallas as pl
from jax.experimental.pallas import tpu as pltpu
from jax.sharding import PartitionSpec as P

HD = 128
SPAN = 8
TILE = 32
NEG = -1e30
SCALE = HD ** (-0.5)
FACTOR = SCALE * 1.4426950408889634
SMALLEST, LARGEST = 2.0 ** -60, 2.0 ** 100
STATE = HD + 8
VROWS = HD + 16
TOTAL, SHIFT = HD, HD + 1
UNIT = 4
STEP = 2
VMEM = 20 * 1024 * 1024


def parent_of(table_ref, segment):
    return table_ref[1 + segment]


def count_of(table_ref, segment):
    return table_ref[1 + (table_ref.shape[0] - 1) // 2 + segment]


def is_ancestor(table_ref, me, source):
    current = me
    hit = jnp.int32(0)
    for _ in range(SPAN - 1):
        current = jnp.where(current >= 0, parent_of(table_ref, jnp.maximum(current, 0)), -1)
        hit = jnp.where(current == source, 1, hit)
    return jnp.where(source >= 0, hit, 0)


def source_of(me, stride, shift, swap):
    offset = me // stride
    base = offset
    if swap:
        base = jnp.where(offset % 2 == 0, offset + 1, offset - 1)
    base = base - shift
    return jnp.where(base >= 0, base * stride + me % stride, -1)


def live_keys(table_ref, me, stride, move):
    if move is None:
        return count_of(table_ref, me)
    source = source_of(me, stride, *move)
    length = count_of(table_ref, jnp.maximum(source, 0))
    return jnp.where(is_ancestor(table_ref, me, source) > 0, length, 0)


def attend(stride, moves, blocks, parts, first, last, table_ref, *refs):
    refs = list(refs)
    n, many = len(moves), len(parts)
    if first:
        q_ref = refs.pop(0)
    else:
        qt_refs = [refs.pop(0) for _ in parts]
        old_refs = [refs.pop(0) for _ in parts]
    kv_refs = [[refs.pop(0) for _ in moves] for _ in parts]
    if last:
        out_ref = refs.pop(0)
    else:
        if first:
            qt_refs = [refs.pop(0) for _ in parts]
        new_refs = [refs.pop(0) for _ in parts]
    k_buf, v_buf, bad_buf = refs

    me = table_ref[0]
    count = count_of(table_ref, me)
    held, _, across_all = qt_refs[0].shape
    rows = v_buf.shape[2] // n
    tiles_max = rows // TILE
    lanes = across_all // tiles_max
    group = lanes // TILE
    tiles = (count + TILE - 1) // TILE
    steps = held // STEP
    head = (pl.program_id(0) % steps) * STEP
    turn_of = pl.program_id(0) // steps
    lengths = [live_keys(table_ref, me, stride, m) for m in moves]

    j_lanes = lax.broadcasted_iota(jnp.int32, (VROWS - HD, rows), 1)
    sub = lax.broadcasted_iota(jnp.int32, (VROWS - HD, rows), 0)

    def fill(i):
        for l in range(n):
            to = slice(l * rows, (l + 1) * rows)
            of = slice(blocks[i][l] * rows, (blocks[i][l] + 1) * rows)
            inside = jnp.where(j_lanes < lengths[l], 1.0, 0.0)
            for h in range(STEP):
                base = pl.multiple_of((head + h) * 2 * HD, 2 * HD)
                k_buf[h, to, :] = kv_refs[i][l][of, pl.ds(base, HD)]
                value = kv_refs[i][l][of, pl.ds(base + HD, HD)]
                v_buf[h, :HD, to] = value.T * inside[:1].astype(jnp.bfloat16)
                v_buf[h, HD:, to] = jnp.where(sub == 0, inside, 0.0).astype(jnp.bfloat16)

    def across(t, k=1):
        if isinstance(t, int):
            return slice(t * lanes, (t + k) * lanes)
        return pl.ds(pl.multiple_of(t * lanes, lanes), k * lanes)

    def down(t):
        if isinstance(t, int):
            return slice(t * TILE, (t + 1) * TILE)
        return pl.ds(pl.multiple_of(t * TILE, TILE), TILE)

    def causal(t, width):
        j = lax.broadcasted_iota(jnp.int32, (rows, width), 0)
        lane = lax.broadcasted_iota(jnp.int32, (rows, width), 1)
        return j <= lane % TILE + (lane // lanes + t) * TILE

    def turned(i, h, t, k):
        if first:
            base = (parts[i] * held + head + h) * group * HD
            for u in range(k):
                heads = [
                    q_ref[down(t + u), pl.ds(pl.multiple_of(base + g * HD, HD), HD)] for g in range(group)
                ]
                qt_refs[i][head + h, :, across(t + u)] = jnp.concatenate(heads, axis=0).T
        return qt_refs[i][head + h, :, across(t, k)]

    def scores(i, h, t, k):
        return jnp.dot(k_buf[h], turned(i, h, t, k), preferred_element_type=jnp.float32)

    def mix(h, weights):
        return jnp.dot(v_buf[h], weights, preferred_element_type=jnp.float32)[:STATE]

    def finish(i, h, t, k, mixed, shift):
        if last:
            result = (mixed[:HD] * (1.0 / mixed[TOTAL:TOTAL + 1])).astype(out_ref.dtype).T
            for u in range(k):
                base = (t + u) * TILE
                live = lax.broadcasted_iota(jnp.int32, (TILE, HD), 0) + base < count
                for g in range(group):
                    at = u * lanes + g * TILE
                    piece = jnp.where(live, result[at:at + TILE].astype(jnp.float32), 0.0)
                    to = (h * group + g) * HD
                    out_ref[down(t + u), to:to + HD] = piece.astype(out_ref.dtype)
        else:
            new_refs[i][head + h, :, across(t, k)] = mixed
            new_refs[i][head + h, SHIFT:SHIFT + 1, across(t, k)] = shift

    def unshifted(i, h, t, k, s):
        w = jnp.exp2(s * FACTOR)
        if first:
            own = jnp.where(causal(t, k * lanes), w[:rows], 0.0)
            w = jnp.concatenate([own, w[rows:]], axis=0) if n > 1 else own
        mixed = mix(h, w.astype(jnp.bfloat16))
        if not first:
            mixed = mixed + old_refs[i][head + h, :, across(t, k)]
        total = mixed[TOTAL:TOTAL + 1]
        good = (total >= SMALLEST) & (total <= LARGEST)
        if not first:
            good = good & (old_refs[i][head + h, SHIFT:SHIFT + 1, across(t, k)] == 0.0)
        bad_buf[h:h + 1, across(t, k)] = jnp.where(good, 0.0, 1.0)
        finish(i, h, t, k, mixed, jnp.zeros((1, k * lanes), jnp.float32))

    def shifted(i, h, t, _):
        s = scores(i, h, t, 1)
        pieces = []
        for l in range(n):
            j = lax.broadcasted_iota(jnp.int32, (rows, lanes), 0)
            allowed = j < lengths[l]
            if moves[l] is None:
                allowed = allowed & causal(t, lanes)
            pieces.append(jnp.where(allowed, s[l * rows:(l + 1) * rows], NEG))
        s = jnp.concatenate(pieces, axis=0)
        top = jnp.max(s, axis=0, keepdims=True)
        if not first:
            before = old_refs[i][head + h, SHIFT:SHIFT + 1, across(t)]
            top = jnp.maximum(top, before)
        w = jnp.exp2((s - top) * FACTOR)
        mixed = mix(h, w.astype(jnp.bfloat16))
        if not first:
            mixed = mixed + old_refs[i][head + h, :, across(t)] * jnp.exp2((before - top) * FACTOR)
        finish(i, h, t, 1, mixed, top)
        return 0

    def run(i, k):
        units = [(i, h, t, min(UNIT, k - t)) for h in range(STEP) for t in range(0, k, UNIT)]
        s = scores(*units[0])
        for at, unit in enumerate(units):
            following = scores(*units[at + 1]) if at + 1 < len(units) else None
            unshifted(*unit, s)
            s = following

    def safely(i):
        for h in range(STEP):
            lax.fori_loop(0, tiles, partial(shifted, i, h), 0)

    def mine(i):
        return turn_of == i if many > 1 else turn_of >= 0

    bad_buf[...] = jnp.zeros(bad_buf.shape, jnp.float32)
    for i in range(many):
        pl.when(mine(i))(partial(fill, i))
    some = sum(lengths) > 0
    for i in range(many):
        for k in range(1, tiles_max + 1):
            pl.when(mine(i) & (tiles == k) & (some | last))(partial(run, i, k))

    def keep(i):
        for h in range(STEP):
            new_refs[i][head + h] = old_refs[i][head + h]

    if not (first or last):
        for i in range(many):
            pl.when(mine(i) & jnp.logical_not(some))(partial(keep, i))
    bad = jnp.max(bad_buf[:STEP, :]) > 0.0
    for i in range(many):
        pl.when(mine(i) & bad)(partial(safely, i))

    if last:
        def clear(t, _):
            out_ref[down(t), :] = jnp.zeros((TILE, out_ref.shape[1]), out_ref.dtype)
            return 0

        lax.fori_loop(tiles, tiles_max, clear, 0)


def levels(stride, table, queries, kv_heads, moves, kvs, state, parts=(0, 1), last=False):
    rows, width = queries.shape
    group = width // HD // kv_heads
    half = kv_heads // 2
    tiles_max = rows // TILE
    lanes = group * TILE
    first = state is None
    steps = half // STEP
    n = len(moves)
    whole = pl.BlockSpec(memory_space=pltpu.VMEM)
    if first:
        operands = [queries]
    else:
        operands = [state[part][0] for part in parts] + [state[part][1] for part in parts]
    operands += [array for part in parts for array, _ in kvs[part]]
    if last:
        out_specs = pl.BlockSpec((rows, STEP * group * HD), lambda k, *_: (0, k))
        out_shape = jax.ShapeDtypeStruct((rows, width), jnp.bfloat16)
    else:
        turned = jax.ShapeDtypeStruct((half, HD, tiles_max * lanes), jnp.bfloat16)
        held = jax.ShapeDtypeStruct((half, STATE, tiles_max * lanes), jnp.float32)
        out_shape = [turned] * (len(parts) if first else 0) + [held] * len(parts)
        out_specs = [whole] * len(out_shape)
    result = pl.pallas_call(
        partial(attend, stride, moves, [[block for _, block in kvs[part]] for part in parts], parts, first, last),
        grid_spec=pltpu.PrefetchScalarGridSpec(
            num_scalar_prefetch=1,
            grid=(len(parts) * steps,),
            in_specs=[whole] * len(operands),
            out_specs=out_specs,
            scratch_shapes=[
                pltpu.VMEM((STEP, n * rows, HD), jnp.bfloat16),
                pltpu.VMEM((STEP, VROWS, n * rows), jnp.bfloat16),
                pltpu.VMEM((8, tiles_max * lanes), jnp.float32),
            ],
        ),
        out_shape=out_shape,
        compiler_params=pltpu.CompilerParams(vmem_limit_bytes=VMEM),
        cost_estimate=pl.CostEstimate(
            flops=2 * rows * rows * width * n * len(parts),
            bytes_accessed=rows * width * len(parts),
            transcendentals=rows * rows * width // HD * n // 2 * len(parts),
        ),
        name="levels_" + str(n) + ("_first" if first else "_last" if last else ""),
    )(table, *operands)
    if last:
        return result
    state = {} if first else dict(state)
    for at, part in enumerate(parts):
        state[part] = (result[at], result[len(parts) + at]) if first else (state[part][0], result[at])
    return state


def per_device(queries, keyvals, parent, counts):
    rows, width = queries.shape
    kv_heads = keyvals.shape[1] // (2 * HD)
    half = kv_heads // 2
    segments = lax.axis_size("tp")
    stride = segments // SPAN
    me = lax.axis_index("tp").reshape(1).astype(jnp.int32)
    table = jnp.concatenate([me, parent, counts])

    def send(x, pairs):
        full = [(a * stride + t, b * stride + t) for a, b in pairs for t in range(stride)]
        return lax.ppermute(x, "tp", full)

    def kernel(moves, kvs, state, **more):
        return levels(stride, table, queries, kv_heads, moves, kvs, state, **more)

    def halves(*arrays):
        return [[(array, part) for array in arrays] for part in (0, 1)]

    swap = [(o, o ^ 1) for o in range(SPAN)]
    up = [(o, (o + 2) % SPAN) for o in range(SPAN)]
    cut = half * 2 * HD
    hold = lax.optimization_barrier
    m1 = [(2, False), (0, True)]
    m2 = [(4, False), (2, True)]
    m3 = [(6, False), (4, True)]
    m4 = [(6, True)]
    both = jnp.concatenate([keyvals[:, :cut], keyvals[:, cut:]], axis=0)
    z1, x1 = send(both, up), send(both, swap)
    state = kernel([None], halves(both), None)
    z1, x1, state = hold((z1, x1, state))
    az1, bz1 = z1[:rows], z1[rows:]
    az2, ax2 = send(az1, up), send(az1, swap)
    bz2, bx2 = send(bz1, up), send(bz1, swap)
    state = kernel(m1, halves(z1, x1), state)
    az2, ax2, state = hold((az2, ax2, state))
    az3, ax3 = send(az2, [(o, o + 2) for o in range(4, SPAN - 2)]), send(az2, swap)
    state = kernel(m2, [[(az2, 0), (ax2, 0)], None], state, parts=(0,))
    bz2, bx2, state = hold((bz2, bx2, state))
    bz3, bx3 = send(bz2, [(o, o + 2) for o in range(4, SPAN - 2)]), send(bz2, swap)
    state = kernel(m2, [None, [(bz2, 0), (bx2, 0)]], state, parts=(1,))
    az3, ax3, state = hold((az3, ax3, state))
    a4 = send(az3, swap)
    state = kernel(m3, [[(az3, 0), (ax3, 0)], None], state, parts=(0,))
    bz3, bx3, state = hold((bz3, bx3, state))
    b4 = send(bx3, [(o, o + 2) for o in range(4, SPAN - 2)])
    state = kernel(m3, [None, [(bz3, 0), (bx3, 0)]], state, parts=(1,))
    a4, b4, state = hold((a4, b4, state))
    return kernel(m4, [[(a4, 0)], [(b4, 0)]], state, last=True)

def solution(mesh):
    in_specs = (P(("rep", "tp"), None), P(("rep", "tp"), None), P("rep"), P("rep"))
    out_specs = P(("rep", "tp"), None)
    return jax.shard_map(
        per_device, mesh=mesh, in_specs=in_specs, out_specs=out_specs, check_vma=False
    )
```

```python
from functools import partial

import jax
import jax.numpy as jnp
from jax import lax
from jax.experimental import pallas as pl
from jax.experimental.pallas import tpu as pltpu
from jax.sharding import PartitionSpec as P

HD = 128
SPAN = 8
TILE = 32
NEG = -1e30
SCALE = HD ** (-0.5)
FACTOR = SCALE * 1.4426950408889634
SMALLEST, LARGEST = 2.0 ** -60, 2.0 ** 100
STATE = HD + 8
VROWS = HD + 16
TOTAL = HD
UNIT = 4
STEP = 2
VMEM = 20 * 1024 * 1024


def parent_of(table_ref, segment):
    return table_ref[1 + segment]


def count_of(table_ref, segment):
    return table_ref[1 + (table_ref.shape[0] - 1) // 2 + segment]


def is_ancestor(table_ref, me, source):
    current = me
    hit = jnp.int32(0)
    for _ in range(SPAN - 1):
        current = jnp.where(current >= 0, parent_of(table_ref, jnp.maximum(current, 0)), -1)
        hit = jnp.where(current == source, 1, hit)
    return jnp.where(source >= 0, hit, 0)


def source_of(me, stride, shift, swap):
    offset = me // stride
    base = offset
    if swap:
        base = jnp.where(offset % 2 == 0, offset + 1, offset - 1)
    base = base - shift
    return jnp.where(base >= 0, base * stride + me % stride, -1)


def live_keys(table_ref, me, stride, move):
    if move is None:
        return count_of(table_ref, me)
    source = source_of(me, stride, *move)
    length = count_of(table_ref, jnp.maximum(source, 0))
    return jnp.where(is_ancestor(table_ref, me, source) > 0, length, 0)


def attend(stride, moves, fold, blocks, parts, first, last, table_ref, *refs):
    refs = list(refs)
    many, n = len(parts), len(fold)
    if first:
        q_ref = refs.pop(0)
    else:
        qt_refs = [refs.pop(0) for _ in parts]
        old_refs = [refs.pop(0) for _ in parts]
    kv_refs = [[refs.pop(0) for _ in moves] for _ in parts]
    if last:
        if parts[0] > 0:
            refs.pop(0)
        out_ref = refs.pop(0)
    else:
        if first:
            qt_refs = [refs.pop(0) for _ in parts]
        new_refs = [refs.pop(0) for _ in parts]
    k_buf, v_buf, bad_buf = refs

    me = table_ref[0]
    count = count_of(table_ref, me)
    held, _, across_all = qt_refs[0].shape
    rows = v_buf.shape[2] // n
    tiles_max = rows // TILE
    lanes = across_all // tiles_max
    group = lanes // TILE
    tiles = (count + TILE - 1) // TILE
    steps = held // STEP
    head = (pl.program_id(0) % steps) * STEP
    turn_of = pl.program_id(0) // steps
    lengths = {l: live_keys(table_ref, me, stride, moves[l]) for l in fold}

    def key_value(i, l, h):
        of = slice(blocks[i][l] * rows, (blocks[i][l] + 1) * rows)
        base = pl.multiple_of((head + h) * 2 * HD, 2 * HD)
        return kv_refs[i][l][of, pl.ds(base, HD)], kv_refs[i][l][of, pl.ds(base + HD, HD)]

    def fill(i):
        j = lax.broadcasted_iota(jnp.int32, (VROWS - HD, rows), 1)
        sub = lax.broadcasted_iota(jnp.int32, (VROWS - HD, rows), 0)
        for at, l in enumerate(fold):
            to = slice(at * rows, (at + 1) * rows)
            inside = jnp.where(j < lengths[l], 1.0, 0.0)
            for h in range(STEP):
                key, value = key_value(i, l, h)
                k_buf[h, to, :] = key
                v_buf[h, :HD, to] = value.T * inside[:1].astype(jnp.bfloat16)
                v_buf[h, HD:, to] = jnp.where(sub == 0, inside, 0.0).astype(jnp.bfloat16)

    def across(t, k=1):
        if isinstance(t, int):
            return slice(t * lanes, (t + k) * lanes)
        return pl.ds(pl.multiple_of(t * lanes, lanes), k * lanes)

    def down(t):
        if isinstance(t, int):
            return slice(t * TILE, (t + 1) * TILE)
        return pl.ds(pl.multiple_of(t * TILE, TILE), TILE)

    def slot(t, shape):
        lane = lax.broadcasted_iota(jnp.int32, shape, 1)
        return lane % TILE + (lane // lanes + t) * TILE

    def turned(i, h, t, k):
        if first:
            base = (parts[i] * held + head + h) * group * HD
            for u in range(k):
                heads = [
                    q_ref[down(t + u), pl.ds(pl.multiple_of(base + g * HD, HD), HD)] for g in range(group)
                ]
                qt_refs[i][head + h, :, across(t + u)] = jnp.concatenate(heads, axis=0).T
        return qt_refs[i][head + h, :, across(t, k)]

    def scores(i, h, t, k):
        return jnp.dot(k_buf[h], turned(i, h, t, k), preferred_element_type=jnp.float32)

    def write(h, t, k, mixed, total):
        live = slot(t, (1, k * lanes)) < count
        result = (mixed * jnp.where(live, 1.0 / total, 0.0)).astype(out_ref.dtype).T
        for u in range(k):
            for g in range(group):
                at = u * lanes + g * TILE
                to = (h * group + g) * HD
                out_ref[down(t + u), to:to + HD] = result[at:at + TILE]

    def unshifted(i, h, t, k, s):
        w = jnp.exp2(s * FACTOR)
        if first:
            j = lax.broadcasted_iota(jnp.int32, (rows, k * lanes), 0)
            w = jnp.where(j <= slot(t, (rows, k * lanes)), w, 0.0)
        mixed = jnp.dot(v_buf[h], w.astype(jnp.bfloat16), preferred_element_type=jnp.float32)[:STATE]
        if not first:
            mixed = mixed + old_refs[i][head + h, :, across(t, k)]
        if last:
            total = mixed[TOTAL:TOTAL + 1]
            good = (total >= SMALLEST) & (total <= LARGEST)
            bad_buf[h:h + 1, across(t, k)] = jnp.where(good, 0.0, 1.0)
            write(h, t, k, mixed[:HD], total)
        else:
            new_refs[i][head + h, :, across(t, k)] = mixed

    def settle(i, k):
        for h in range(STEP):
            mixed = old_refs[i][head + h, :, across(0, k)]
            total = mixed[TOTAL:TOTAL + 1]
            good = (total >= SMALLEST) & (total <= LARGEST)
            bad_buf[h:h + 1, across(0, k)] = jnp.where(good, 0.0, 1.0)
            write(h, 0, k, mixed[:HD], total)

    def run(i, k):
        units = [(i, h, t, min(UNIT, k - t)) for h in range(STEP) for t in range(0, k, UNIT)]
        s = scores(*units[0])
        for at, unit in enumerate(units):
            following = scores(*units[at + 1]) if at + 1 < len(units) else None
            unshifted(*unit, s)
            s = following

    def shifted(i, h, t, _):
        q = qt_refs[i][head + h, :, across(t)]
        j = lax.broadcasted_iota(jnp.int32, (rows, lanes), 0)
        pieces = []
        for l, move in enumerate(moves):
            s = jnp.dot(key_value(i, l, h)[0], q, preferred_element_type=jnp.float32)
            allowed = j < live_keys(table_ref, me, stride, move)
            if move is None:
                allowed = allowed & (j <= slot(t, (rows, lanes)))
            pieces.append(jnp.where(allowed, s, NEG))
        top = jnp.max(pieces[0], axis=0, keepdims=True)
        for s in pieces[1:]:
            top = jnp.maximum(top, jnp.max(s, axis=0, keepdims=True))
        mixed = jnp.zeros((HD, lanes), jnp.float32)
        total = jnp.zeros((1, lanes), jnp.float32)
        for l, s in enumerate(pieces):
            w = jnp.exp2((s - top) * FACTOR)
            total = total + jnp.sum(w, axis=0, keepdims=True)
            value_t = key_value(i, l, h)[1].T
            mixed = mixed + jnp.dot(value_t, w.astype(jnp.bfloat16), preferred_element_type=jnp.float32)
        write(h, t, 1, mixed, total)
        return 0

    def safely(i):
        for h in range(STEP):
            lax.fori_loop(0, tiles, partial(shifted, i, h), 0)

    def keep(i):
        for h in range(STEP):
            new_refs[i][head + h] = old_refs[i][head + h]

    some = sum(lengths.values()) > 0
    for i in range(many):
        here = turn_of == i if many > 1 else count > 0
        mine = here & some
        pl.when(mine)(partial(fill, i))
        if last:
            bad_buf[...] = jnp.zeros(bad_buf.shape, jnp.float32)
        for k in range(1, tiles_max + 1):
            pl.when(mine & (tiles == k))(partial(run, i, k))
            if last:
                pl.when(here & jnp.logical_not(some) & (tiles == k))(partial(settle, i, k))
        if last:
            pl.when(here & (jnp.max(bad_buf[:STEP, :]) > 0.0))(partial(safely, i))
        elif not first:
            pl.when(here & jnp.logical_not(some))(partial(keep, i))

    if last:
        def clear(t, _):
            out_ref[down(t), :] = jnp.zeros((TILE, out_ref.shape[1]), out_ref.dtype)
            return 0

        lax.fori_loop(tiles, tiles_max, clear, 0)


def levels(stride, table, queries, kv_heads, moves, kvs, state, parts=(0, 1), fold=None, last=False, into=None, begin=False):
    rows, width = queries.shape
    group = width // HD // kv_heads
    half = kv_heads // 2
    tiles_max = rows // TILE
    lanes = group * TILE
    first = state is None or begin
    steps = half // STEP
    fold = list(range(len(moves))) if fold is None else fold
    n, many = len(fold), len(parts)
    whole = pl.BlockSpec(memory_space=pltpu.VMEM)
    if first:
        operands = [queries]
    else:
        operands = [state[part][0] for part in parts] + [state[part][1] for part in parts]
    operands += [array for part in parts for array, _ in kvs[part]]
    specs = [whole] * len(operands)
    aliases = {}
    if into is not None:
        specs.append(pl.BlockSpec(memory_space=pl.ANY))
        aliases = {1 + len(operands): 0}
        operands.append(into)
    if last:
        out_specs = pl.BlockSpec((rows, STEP * group * HD), lambda k, *_: (0, k + parts[0] * steps))
        out_shape = jax.ShapeDtypeStruct((rows, width), jnp.bfloat16)
    else:
        turned = jax.ShapeDtypeStruct((half, HD, tiles_max * lanes), jnp.bfloat16)
        held = jax.ShapeDtypeStruct((half, STATE, tiles_max * lanes), jnp.float32)
        out_shape = [turned] * (many if first else 0) + [held] * many
        out_specs = [whole] * len(out_shape)
    result = pl.pallas_call(
        partial(attend, stride, moves, fold, [[block for _, block in kvs[part]] for part in parts], parts, first, last),
        grid_spec=pltpu.PrefetchScalarGridSpec(
            num_scalar_prefetch=1,
            grid=(many * steps,),
            in_specs=specs,
            out_specs=out_specs,
            scratch_shapes=[
                pltpu.VMEM((STEP, n * rows, HD), jnp.bfloat16),
                pltpu.VMEM((STEP, VROWS, n * rows), jnp.bfloat16),
                pltpu.VMEM((8, tiles_max * lanes), jnp.float32),
            ],
        ),
        out_shape=out_shape,
        input_output_aliases=aliases,
        compiler_params=pltpu.CompilerParams(vmem_limit_bytes=VMEM),
        cost_estimate=pl.CostEstimate(
            flops=2 * rows * rows * width * n * many,
            bytes_accessed=rows * width * many,
            transcendentals=rows * rows * width // HD * n // 2 * many,
        ),
        name="levels_" + str(n) + ("_first" if first else "_last" if last else ""),
    )(table, *operands)
    if last:
        return result
    state = dict(state or {})
    for at, part in enumerate(parts):
        state[part] = (result[at], result[many + at]) if first else (state[part][0], result[at])
    return state


def per_device(queries, keyvals, parent, counts):
    rows, width = queries.shape
    kv_heads = keyvals.shape[1] // (2 * HD)
    half = kv_heads // 2
    segments = lax.axis_size("tp")
    stride = segments // SPAN
    me = lax.axis_index("tp").reshape(1).astype(jnp.int32)
    table = jnp.concatenate([me, parent, counts])

    def send(x, pairs):
        full = [(a * stride + t, b * stride + t) for a, b in pairs for t in range(stride)]
        return lax.ppermute(x, "tp", full)

    def kernel(moves, kvs, state, **more):
        return levels(stride, table, queries, kv_heads, moves, kvs, state, **more)

    def halves(*arrays):
        return [[(array, part) for array in arrays] for part in (0, 1)]

    swap = [(o, o ^ 1) for o in range(SPAN)]
    up = [(o, (o + 2) % SPAN) for o in range(SPAN)]
    swap3 = [(o, o ^ 1) for o in range(4, SPAN)]
    swap4 = [(o, o ^ 1) for o in range(6, SPAN)]
    up3 = [(o, o + 2) for o in range(4, SPAN - 2)]
    cut = half * 2 * HD
    hold = lax.optimization_barrier
    m1 = [(2, False), (0, True)]
    m2 = [(4, False), (2, True)]
    m3 = [(6, False), (4, True)]
    m4 = [(6, True)]
    every = [None] + m1 + m2 + m3 + m4
    a, b = keyvals[:, :cut], keyvals[:, cut:]
    ax1, az1 = send(a, swap), send(a, up)
    bx1, bz1 = send(b, swap), send(b, up)
    state = kernel([None], [[(a, 0)], None], None, parts=(0,))
    az1, ax1, state = hold((az1, ax1, state))
    ax2 = send(az1, swap)
    az2 = send(az1, up)
    state = kernel([None], [None, [(b, 0)]], state, parts=(1,), begin=True)
    bz1, bx1, state = hold((bz1, bx1, state))
    bx2 = send(bz1, swap)
    bz2 = send(bz1, up)
    state = kernel(m1, [[(az1, 0), (ax1, 0)], [(bz1, 0), (bx1, 0)]], state)
    az2, ax2, state = hold((az2, ax2, state))
    ax3 = send(az2, swap)
    az3 = send(az2, up3)
    state = kernel(m2, [[(az2, 0), (ax2, 0)], None], state, parts=(0,))
    bz2, bx2, state = hold((bz2, bx2, state))
    bx3 = send(bz2, swap)
    bz3 = send(bz2, up3)
    state = kernel(m2, [None, [(bz2, 0), (bx2, 0)]], state, parts=(1,))
    az3, ax3, state = hold((az3, ax3, state))
    a4 = send(az3, swap)
    state = kernel(m3, [[(az3, 0), (ax3, 0)], None], state, parts=(0,))
    bz3, bx3, state = hold((bz3, bx3, state))
    b4 = send(bx3, up3)
    state = kernel(m3, [None, [(bz3, 0), (bx3, 0)]], state, parts=(1,))
    of_a = [(a, 0), (az1, 0), (ax1, 0), (az2, 0), (ax2, 0), (az3, 0), (ax3, 0), (a4, 0)]
    of_b = [(b, 0), (bz1, 0), (bx1, 0), (bz2, 0), (bx2, 0), (bz3, 0), (bx3, 0), (b4, 0)]
    out = kernel(every, [of_a, None], state, parts=(0,), fold=[7], last=True)
    return kernel(every, [None, of_b], state, parts=(1,), fold=[7], last=True, into=out)

def solution(mesh):
    in_specs = (P(("rep", "tp"), None), P(("rep", "tp"), None), P("rep"), P("rep"))
    out_specs = P(("rep", "tp"), None)
    return jax.shard_map(
        per_device, mesh=mesh, in_specs=in_specs, out_specs=out_specs, check_vma=False
    )
```

```python
from functools import partial

import jax
import jax.numpy as jnp
from jax import lax
from jax.experimental import pallas as pl
from jax.experimental.pallas import tpu as pltpu
from jax.sharding import PartitionSpec as P

HD = 128
SPAN = 8
TILE = 32
NEG = -1e30
SCALE = HD ** (-0.5)
FACTOR = SCALE * 1.4426950408889634
SMALLEST, LARGEST = 2.0 ** -60, 2.0 ** 100
STATE = HD + 8
VROWS = HD + 16
TOTAL = HD
UNIT = 4
STEP = 2
VMEM = 20 * 1024 * 1024


def parent_of(table_ref, segment):
    return table_ref[1 + segment]


def count_of(table_ref, segment):
    return table_ref[1 + (table_ref.shape[0] - 1) // 2 + segment]


def is_ancestor(table_ref, me, source):
    current = me
    hit = jnp.int32(0)
    for _ in range(SPAN - 1):
        current = jnp.where(current >= 0, parent_of(table_ref, jnp.maximum(current, 0)), -1)
        hit = jnp.where(current == source, 1, hit)
    return jnp.where(source >= 0, hit, 0)


def source_of(me, stride, shift, swap):
    offset = me // stride
    base = offset
    if swap:
        base = jnp.where(offset % 2 == 0, offset + 1, offset - 1)
    base = base - shift
    return jnp.where(base >= 0, base * stride + me % stride, -1)


def live_keys(table_ref, me, stride, move):
    if move is None:
        return count_of(table_ref, me)
    source = source_of(me, stride, *move)
    length = count_of(table_ref, jnp.maximum(source, 0))
    return jnp.where(is_ancestor(table_ref, me, source) > 0, length, 0)


def attend(stride, moves, fold, blocks, parts, first, last, table_ref, *refs):
    refs = list(refs)
    many, n = len(parts), len(fold)
    if first:
        q_ref = refs.pop(0)
    else:
        qt_refs = [refs.pop(0) for _ in parts]
        old_refs = [refs.pop(0) for _ in parts]
    kv_refs = [[refs.pop(0) for _ in moves] for _ in parts]
    if last:
        if parts[0] > 0:
            refs.pop(0)
        out_ref = refs.pop(0)
    else:
        if first:
            qt_refs = [refs.pop(0) for _ in parts]
        new_refs = [refs.pop(0) for _ in parts]
    k_buf, v_buf, bad_buf = refs

    me = table_ref[0]
    count = count_of(table_ref, me)
    held, _, across_all = qt_refs[0].shape
    rows = v_buf.shape[2] // n
    tiles_max = rows // TILE
    lanes = across_all // tiles_max
    group = lanes // TILE
    tiles = (count + TILE - 1) // TILE
    steps = held // STEP
    head = (pl.program_id(0) % steps) * STEP
    turn_of = pl.program_id(0) // steps
    lengths = {l: live_keys(table_ref, me, stride, moves[l]) for l in fold}

    def key_value(i, l, h):
        of = slice(blocks[i][l] * rows, (blocks[i][l] + 1) * rows)
        base = pl.multiple_of((head + h) * 2 * HD, 2 * HD)
        return kv_refs[i][l][of, pl.ds(base, HD)], kv_refs[i][l][of, pl.ds(base + HD, HD)]

    def fill(i):
        j = lax.broadcasted_iota(jnp.int32, (VROWS - HD, rows), 1)
        sub = lax.broadcasted_iota(jnp.int32, (VROWS - HD, rows), 0)
        for at, l in enumerate(fold):
            to = slice(at * rows, (at + 1) * rows)
            inside = jnp.where(j < lengths[l], 1.0, 0.0)
            for h in range(STEP):
                key, value = key_value(i, l, h)
                k_buf[h, to, :] = key
                v_buf[h, :HD, to] = value.T * inside[:1].astype(jnp.bfloat16)
                v_buf[h, HD:, to] = jnp.where(sub == 0, inside, 0.0).astype(jnp.bfloat16)

    def across(t, k=1):
        if isinstance(t, int):
            return slice(t * lanes, (t + k) * lanes)
        return pl.ds(pl.multiple_of(t * lanes, lanes), k * lanes)

    def down(t):
        if isinstance(t, int):
            return slice(t * TILE, (t + 1) * TILE)
        return pl.ds(pl.multiple_of(t * TILE, TILE), TILE)

    def slot(t, shape):
        lane = lax.broadcasted_iota(jnp.int32, shape, 1)
        return lane % TILE + (lane // lanes + t) * TILE

    def turned(i, h, t, k):
        if first:
            base = (parts[i] * held + head + h) * group * HD
            for u in range(k):
                heads = [
                    q_ref[down(t + u), pl.ds(pl.multiple_of(base + g * HD, HD), HD)] for g in range(group)
                ]
                qt_refs[i][head + h, :, across(t + u)] = jnp.concatenate(heads, axis=0).T
        return qt_refs[i][head + h, :, across(t, k)]

    def scores(i, h, t, k):
        return jnp.dot(k_buf[h], turned(i, h, t, k), preferred_element_type=jnp.float32)

    def write(h, t, k, mixed, total):
        live = slot(t, (1, k * lanes)) < count
        result = (mixed * jnp.where(live, 1.0 / total, 0.0)).astype(out_ref.dtype).T
        for u in range(k):
            for g in range(group):
                at = u * lanes + g * TILE
                to = (h * group + g) * HD
                out_ref[down(t + u), to:to + HD] = result[at:at + TILE]

    def unshifted(i, h, t, k, s):
        w = jnp.exp2(s * FACTOR)
        if first:
            j = lax.broadcasted_iota(jnp.int32, (rows, k * lanes), 0)
            own = jnp.where(j <= slot(t, (rows, k * lanes)), w[:rows], 0.0)
            w = jnp.concatenate([own, w[rows:]], axis=0) if n > 1 else own
        mixed = jnp.dot(v_buf[h], w.astype(jnp.bfloat16), preferred_element_type=jnp.float32)[:STATE]
        if not first:
            mixed = mixed + old_refs[i][head + h, :, across(t, k)]
        if last:
            total = mixed[TOTAL:TOTAL + 1]
            good = (total >= SMALLEST) & (total <= LARGEST)
            bad_buf[h:h + 1, across(t, k)] = jnp.where(good, 0.0, 1.0)
            write(h, t, k, mixed[:HD], total)
        else:
            new_refs[i][head + h, :, across(t, k)] = mixed

    def settle(i, k):
        for h in range(STEP):
            mixed = old_refs[i][head + h, :, across(0, k)]
            total = mixed[TOTAL:TOTAL + 1]
            good = (total >= SMALLEST) & (total <= LARGEST)
            bad_buf[h:h + 1, across(0, k)] = jnp.where(good, 0.0, 1.0)
            write(h, 0, k, mixed[:HD], total)

    def run(i, k):
        units = [(i, h, t, min(UNIT, k - t)) for h in range(STEP) for t in range(0, k, UNIT)]
        s = scores(*units[0])
        for at, unit in enumerate(units):
            following = scores(*units[at + 1]) if at + 1 < len(units) else None
            unshifted(*unit, s)
            s = following

    def shifted(i, h, t, _):
        q = qt_refs[i][head + h, :, across(t)]
        j = lax.broadcasted_iota(jnp.int32, (rows, lanes), 0)
        pieces = []
        for l, move in enumerate(moves):
            s = jnp.dot(key_value(i, l, h)[0], q, preferred_element_type=jnp.float32)
            allowed = j < live_keys(table_ref, me, stride, move)
            if move is None:
                allowed = allowed & (j <= slot(t, (rows, lanes)))
            pieces.append(jnp.where(allowed, s, NEG))
        top = jnp.max(pieces[0], axis=0, keepdims=True)
        for s in pieces[1:]:
            top = jnp.maximum(top, jnp.max(s, axis=0, keepdims=True))
        mixed = jnp.zeros((HD, lanes), jnp.float32)
        total = jnp.zeros((1, lanes), jnp.float32)
        for l, s in enumerate(pieces):
            w = jnp.exp2((s - top) * FACTOR)
            total = total + jnp.sum(w, axis=0, keepdims=True)
            value_t = key_value(i, l, h)[1].T
            mixed = mixed + jnp.dot(value_t, w.astype(jnp.bfloat16), preferred_element_type=jnp.float32)
        write(h, t, 1, mixed, total)
        return 0

    def safely(i):
        for h in range(STEP):
            lax.fori_loop(0, tiles, partial(shifted, i, h), 0)

    def keep(i):
        for h in range(STEP):
            new_refs[i][head + h] = old_refs[i][head + h]

    some = sum(lengths.values()) > 0
    for i in range(many):
        here = turn_of == i if many > 1 else count > 0
        mine = here & some
        pl.when(mine)(partial(fill, i))
        if last:
            bad_buf[...] = jnp.zeros(bad_buf.shape, jnp.float32)
        for k in range(1, tiles_max + 1):
            pl.when(mine & (tiles == k))(partial(run, i, k))
            if last:
                pl.when(here & jnp.logical_not(some) & (tiles == k))(partial(settle, i, k))
        if last:
            pl.when(here & (jnp.max(bad_buf[:STEP, :]) > 0.0))(partial(safely, i))
        elif not first:
            pl.when(here & jnp.logical_not(some))(partial(keep, i))

    if last:
        def clear(t, _):
            out_ref[down(t), :] = jnp.zeros((TILE, out_ref.shape[1]), out_ref.dtype)
            return 0

        lax.fori_loop(tiles, tiles_max, clear, 0)


def levels(stride, table, queries, kv_heads, moves, kvs, state, parts=(0, 1), fold=None, last=False, into=None, begin=False):
    rows, width = queries.shape
    group = width // HD // kv_heads
    half = kv_heads // 2
    tiles_max = rows // TILE
    lanes = group * TILE
    first = state is None or begin
    steps = half // STEP
    fold = list(range(len(moves))) if fold is None else fold
    n, many = len(fold), len(parts)
    whole = pl.BlockSpec(memory_space=pltpu.VMEM)
    if first:
        operands = [queries]
    else:
        operands = [state[part][0] for part in parts] + [state[part][1] for part in parts]
    operands += [array for part in parts for array, _ in kvs[part]]
    specs = [whole] * len(operands)
    aliases = {}
    if into is not None:
        specs.append(pl.BlockSpec(memory_space=pl.ANY))
        aliases = {1 + len(operands): 0}
        operands.append(into)
    if last:
        out_specs = pl.BlockSpec((rows, STEP * group * HD), lambda k, *_: (0, k + parts[0] * steps))
        out_shape = jax.ShapeDtypeStruct((rows, width), jnp.bfloat16)
    else:
        turned = jax.ShapeDtypeStruct((half, HD, tiles_max * lanes), jnp.bfloat16)
        held = jax.ShapeDtypeStruct((half, STATE, tiles_max * lanes), jnp.float32)
        out_shape = [turned] * (many if first else 0) + [held] * many
        out_specs = [whole] * len(out_shape)
    result = pl.pallas_call(
        partial(attend, stride, moves, fold, [[block for _, block in kvs[part]] for part in parts], parts, first, last),
        grid_spec=pltpu.PrefetchScalarGridSpec(
            num_scalar_prefetch=1,
            grid=(many * steps,),
            in_specs=specs,
            out_specs=out_specs,
            scratch_shapes=[
                pltpu.VMEM((STEP, n * rows, HD), jnp.bfloat16),
                pltpu.VMEM((STEP, VROWS, n * rows), jnp.bfloat16),
                pltpu.VMEM((8, tiles_max * lanes), jnp.float32),
            ],
        ),
        out_shape=out_shape,
        input_output_aliases=aliases,
        compiler_params=pltpu.CompilerParams(vmem_limit_bytes=VMEM),
        cost_estimate=pl.CostEstimate(
            flops=2 * rows * rows * width * n * many,
            bytes_accessed=rows * width * many,
            transcendentals=rows * rows * width // HD * n // 2 * many,
        ),
        name="levels_" + str(n) + ("_first" if first else "_last" if last else ""),
    )(table, *operands)
    if last:
        return result
    state = dict(state or {})
    for at, part in enumerate(parts):
        state[part] = (result[at], result[many + at]) if first else (state[part][0], result[at])
    return state


def per_device(queries, keyvals, parent, counts):
    rows, width = queries.shape
    kv_heads = keyvals.shape[1] // (2 * HD)
    half = kv_heads // 2
    segments = lax.axis_size("tp")
    stride = segments // SPAN
    me = lax.axis_index("tp").reshape(1).astype(jnp.int32)
    table = jnp.concatenate([me, parent, counts])

    def send(x, pairs):
        full = [(a * stride + t, b * stride + t) for a, b in pairs for t in range(stride)]
        return lax.ppermute(x, "tp", full)

    def kernel(moves, kvs, state, **more):
        return levels(stride, table, queries, kv_heads, moves, kvs, state, **more)

    def halves(*arrays):
        return [[(array, part) for array in arrays] for part in (0, 1)]

    swap = [(o, o ^ 1) for o in range(SPAN)]
    up = [(o, (o + 2) % SPAN) for o in range(SPAN)]
    swap3 = [(o, o ^ 1) for o in range(4, SPAN)]
    swap4 = [(o, o ^ 1) for o in range(6, SPAN)]
    up3 = [(o, o + 2) for o in range(4, SPAN - 2)]
    cut = half * 2 * HD
    hold = lax.optimization_barrier
    m1 = [(2, False), (0, True)]
    m2 = [(4, False), (2, True)]
    m3 = [(6, False), (4, True)]
    m4 = [(6, True)]
    every = [None] + m1 + m2 + m3 + m4
    a, b = keyvals[:, :cut], keyvals[:, cut:]
    ax1, az1 = send(a, swap), send(a, up)
    bx1, bz1 = send(b, swap), send(b, up)
    state = kernel([None], [[(a, 0)], None], None, parts=(0,))
    az1, ax1, state = hold((az1, ax1, state))
    ax2 = send(az1, swap)
    az2 = send(az1, up)
    state = kernel([None], [None, [(b, 0)]], state, parts=(1,), begin=True)
    bz1, bx1, state = hold((bz1, bx1, state))
    bx2 = send(bz1, swap)
    bz2 = send(bz1, up)
    state = kernel(m1, [[(az1, 0), (ax1, 0)], [(bz1, 0), (bx1, 0)]], state, parts=(0,))
    az2, ax2, state = hold((az2, ax2, state))
    ax3 = send(az2, swap)
    az3 = send(az2, up3)
    state = kernel(m2, [[(az2, 0), (ax2, 0)], None], state, parts=(0,))
    bz2, bx2, state = hold((bz2, bx2, state))
    bx3 = send(bz2, swap)
    bz3 = send(bz2, up3)
    state = kernel(m1 + m2, [None, [(bz1, 0), (bx1, 0), (bz2, 0), (bx2, 0)]], state, parts=(1,))
    az3, ax3, state = hold((az3, ax3, state))
    a4 = send(az3, swap)
    state = kernel(m3, [[(az3, 0), (ax3, 0)], None], state, parts=(0,))
    bz3, bx3, state = hold((bz3, bx3, state))
    b4 = send(bx3, up3)
    state = kernel(m3, [None, [(bz3, 0), (bx3, 0)]], state, parts=(1,))
    of_a = [(a, 0), (az1, 0), (ax1, 0), (az2, 0), (ax2, 0), (az3, 0), (ax3, 0), (a4, 0)]
    of_b = [(b, 0), (bz1, 0), (bx1, 0), (bz2, 0), (bx2, 0), (bz3, 0), (bx3, 0), (b4, 0)]
    out = kernel(every, [of_a, None], state, parts=(0,), fold=[7], last=True)
    return kernel(every, [None, of_b], state, parts=(1,), fold=[7], last=True, into=out)

def solution(mesh):
    in_specs = (P(("rep", "tp"), None), P(("rep", "tp"), None), P("rep"), P("rep"))
    out_specs = P(("rep", "tp"), None)
    return jax.shard_map(
        per_device, mesh=mesh, in_specs=in_specs, out_specs=out_specs, check_vma=False
    )
```

```python
from functools import partial

import jax
import jax.numpy as jnp
from jax import lax
from jax.experimental import pallas as pl
from jax.experimental.pallas import tpu as pltpu
from jax.sharding import PartitionSpec as P

HD = 128
SPAN = 8
TILE = 32
NEG = -1e30
SCALE = HD ** (-0.5)
FACTOR = SCALE * 1.4426950408889634
SMALLEST, LARGEST = 2.0 ** -60, 2.0 ** 100
STATE = HD + 8
VROWS = HD + 16
TOTAL = HD
UNIT = 4
STEP = 2
VMEM = 20 * 1024 * 1024


def parent_of(table_ref, segment):
    return table_ref[1 + segment]


def count_of(table_ref, segment):
    return table_ref[1 + (table_ref.shape[0] - 1) // 2 + segment]


def is_ancestor(table_ref, me, source):
    current = me
    hit = jnp.int32(0)
    for _ in range(SPAN - 1):
        current = jnp.where(current >= 0, parent_of(table_ref, jnp.maximum(current, 0)), -1)
        hit = jnp.where(current == source, 1, hit)
    return jnp.where(source >= 0, hit, 0)


def source_of(me, stride, shift, swap):
    offset = me // stride
    base = offset
    if swap:
        base = jnp.where(offset % 2 == 0, offset + 1, offset - 1)
    base = base - shift
    return jnp.where(base >= 0, base * stride + me % stride, -1)


def live_keys(table_ref, me, stride, move):
    if move is None:
        return count_of(table_ref, me)
    source = source_of(me, stride, *move)
    length = count_of(table_ref, jnp.maximum(source, 0))
    return jnp.where(is_ancestor(table_ref, me, source) > 0, length, 0)


def attend(stride, moves, fold, blocks, parts, first, last, table_ref, *refs):
    refs = list(refs)
    many, n = len(parts), len(fold)
    if first:
        q_ref = refs.pop(0)
    else:
        qt_refs = [refs.pop(0) for _ in parts]
        old_refs = [refs.pop(0) for _ in parts]
    kv_refs = [[refs.pop(0) for _ in moves] for _ in parts]
    if last:
        if parts[0] > 0:
            refs.pop(0)
        out_ref = refs.pop(0)
    else:
        if first:
            qt_refs = [refs.pop(0) for _ in parts]
        new_refs = [refs.pop(0) for _ in parts]
    k_buf, v_buf, bad_buf = refs[:3]
    if last:
        out_buf, sems = refs[3:]

    me = table_ref[0]
    count = count_of(table_ref, me)
    held, _, across_all = qt_refs[0].shape
    rows = v_buf.shape[2] // n
    tiles_max = rows // TILE
    lanes = across_all // tiles_max
    group = lanes // TILE
    tiles = (count + TILE - 1) // TILE
    steps = held // STEP
    head = (pl.program_id(0) % steps) * STEP
    turn_of = pl.program_id(0) // steps
    lengths = {l: live_keys(table_ref, me, stride, moves[l]) for l in fold}

    def key_value(i, l, h):
        of = slice(blocks[i][l] * rows, (blocks[i][l] + 1) * rows)
        base = pl.multiple_of((head + h) * 2 * HD, 2 * HD)
        return kv_refs[i][l][of, pl.ds(base, HD)], kv_refs[i][l][of, pl.ds(base + HD, HD)]

    def fill(i):
        j = lax.broadcasted_iota(jnp.int32, (VROWS - HD, rows), 1)
        sub = lax.broadcasted_iota(jnp.int32, (VROWS - HD, rows), 0)
        for at, l in enumerate(fold):
            to = slice(at * rows, (at + 1) * rows)
            inside = jnp.where(j < lengths[l], 1.0, 0.0)
            for h in range(STEP):
                key, value = key_value(i, l, h)
                k_buf[h, to, :] = key
                v_buf[h, :HD, to] = value.T * inside[:1].astype(jnp.bfloat16)
                v_buf[h, HD:, to] = jnp.where(sub == 0, inside, 0.0).astype(jnp.bfloat16)

    def across(t, k=1):
        if isinstance(t, int):
            return slice(t * lanes, (t + k) * lanes)
        return pl.ds(pl.multiple_of(t * lanes, lanes), k * lanes)

    def down(t):
        if isinstance(t, int):
            return slice(t * TILE, (t + 1) * TILE)
        return pl.ds(pl.multiple_of(t * TILE, TILE), TILE)

    def slot(t, shape):
        lane = lax.broadcasted_iota(jnp.int32, shape, 1)
        return lane % TILE + (lane // lanes + t) * TILE

    def turned(i, h, t, k):
        if first:
            base = (parts[i] * held + head + h) * group * HD
            for u in range(k):
                heads = [
                    q_ref[down(t + u), pl.ds(pl.multiple_of(base + g * HD, HD), HD)] for g in range(group)
                ]
                qt_refs[i][head + h, :, across(t + u)] = jnp.concatenate(heads, axis=0).T
        return qt_refs[i][head + h, :, across(t, k)]

    def scores(i, h, t, k):
        return jnp.dot(k_buf[h], turned(i, h, t, k), preferred_element_type=jnp.float32)

    def write(h, t, k, mixed, total):
        live = slot(t, (1, k * lanes)) < count
        result = (mixed * jnp.where(live, 1.0 / total, 0.0)).astype(out_ref.dtype).T
        for u in range(k):
            for g in range(group):
                at = u * lanes + g * TILE
                to = pl.multiple_of((head + h) * group * HD + g * HD, HD)
                out_buf[down(t + u), pl.ds(to, HD)] = result[at:at + TILE]

    def leave(h):
        size = group * HD
        return pltpu.make_async_copy(
            out_buf.at[:, pl.ds(pl.multiple_of(h * size, size), size)],
            out_ref.at[:, pl.ds(pl.multiple_of((parts[0] * held + h) * size, size), size)],
            sems.at[h],
        )

    def unshifted(i, h, t, k, s):
        w = jnp.exp2(s * FACTOR)
        if first:
            j = lax.broadcasted_iota(jnp.int32, (rows, k * lanes), 0)
            own = jnp.where(j <= slot(t, (rows, k * lanes)), w[:rows], 0.0)
            w = jnp.concatenate([own, w[rows:]], axis=0) if n > 1 else own
        mixed = jnp.dot(v_buf[h], w.astype(jnp.bfloat16), preferred_element_type=jnp.float32)[:STATE]
        if not first:
            mixed = mixed + old_refs[i][head + h, :, across(t, k)]
        if last:
            total = mixed[TOTAL:TOTAL + 1]
            good = (total >= SMALLEST) & (total <= LARGEST)
            bad_buf[pl.ds(head + h, 1), across(t, k)] = jnp.where(good, 0.0, 1.0)
            write(h, t, k, mixed[:HD], total)
        else:
            new_refs[i][head + h, :, across(t, k)] = mixed

    def settle(i, k):
        for h in range(STEP):
            mixed = old_refs[i][head + h, :, across(0, k)]
            total = mixed[TOTAL:TOTAL + 1]
            good = (total >= SMALLEST) & (total <= LARGEST)
            bad_buf[pl.ds(head + h, 1), across(0, k)] = jnp.where(good, 0.0, 1.0)
            write(h, 0, k, mixed[:HD], total)
            leave(head + h).start()

    def run(i, k):
        units = [(i, h, t, min(UNIT, k - t)) for h in range(STEP) for t in range(0, k, UNIT)]
        s = scores(*units[0])
        for at, unit in enumerate(units):
            following = scores(*units[at + 1]) if at + 1 < len(units) else None
            unshifted(*unit, s)
            if last and (at + 1 == len(units) or units[at + 1][1] != unit[1]):
                leave(head + unit[1]).start()
            s = following

    def shifted(i, h, t, _):
        q = qt_refs[i][head + h, :, across(t)]
        j = lax.broadcasted_iota(jnp.int32, (rows, lanes), 0)
        pieces = []
        for l, move in enumerate(moves):
            s = jnp.dot(key_value(i, l, h)[0], q, preferred_element_type=jnp.float32)
            allowed = j < live_keys(table_ref, me, stride, move)
            if move is None:
                allowed = allowed & (j <= slot(t, (rows, lanes)))
            pieces.append(jnp.where(allowed, s, NEG))
        top = jnp.max(pieces[0], axis=0, keepdims=True)
        for s in pieces[1:]:
            top = jnp.maximum(top, jnp.max(s, axis=0, keepdims=True))
        mixed = jnp.zeros((HD, lanes), jnp.float32)
        total = jnp.zeros((1, lanes), jnp.float32)
        for l, s in enumerate(pieces):
            w = jnp.exp2((s - top) * FACTOR)
            total = total + jnp.sum(w, axis=0, keepdims=True)
            value_t = key_value(i, l, h)[1].T
            mixed = mixed + jnp.dot(value_t, w.astype(jnp.bfloat16), preferred_element_type=jnp.float32)
        write(h, t, 1, mixed, total)
        return 0

    def safely(i):
        def again(h, _):
            leave(h).wait()
            lax.fori_loop(0, tiles, partial(shifted, i, h - head), 0)
            leave(h).start()
            return 0

        lax.fori_loop(0, held, again, 0)

    def keep(i):
        for h in range(STEP):
            new_refs[i][head + h] = old_refs[i][head + h]

    if last:
        def clear(t, _):
            size = STEP * group * HD
            part = pl.ds(pl.multiple_of(head * group * HD, size), size)
            out_buf[down(t), part] = jnp.zeros((TILE, size), out_buf.dtype)
            return 0

        lax.fori_loop(tiles, tiles_max, clear, 0)

    some = sum(lengths.values()) > 0
    for i in range(many):
        here = turn_of == i if many > 1 else count > 0
        mine = here & some
        pl.when(mine)(partial(fill, i))
        if last:
            @pl.when(pl.program_id(0) == 0)
            def _():
                bad_buf[...] = jnp.zeros(bad_buf.shape, jnp.float32)

        for k in range(1, tiles_max + 1):
            pl.when(mine & (tiles == k))(partial(run, i, k))
            if last:
                pl.when(here & jnp.logical_not(some) & (tiles == k))(partial(settle, i, k))
        if last:
            @pl.when(pl.program_id(0) == steps - 1)
            def _():
                pl.when(here & (jnp.max(bad_buf[...]) > 0.0))(partial(safely, i))

        elif not first:
            pl.when(here & jnp.logical_not(some))(partial(keep, i))

    if last:
        @pl.when(pl.program_id(0) == steps - 1)
        def _():
            for h in range(held):
                leave(h).wait()


def levels(stride, table, queries, kv_heads, moves, kvs, state, parts=(0, 1), fold=None, last=False, into=None, begin=False):
    rows, width = queries.shape
    group = width // HD // kv_heads
    half = kv_heads // 2
    tiles_max = rows // TILE
    lanes = group * TILE
    first = state is None or begin
    steps = half // STEP
    fold = list(range(len(moves))) if fold is None else fold
    n, many = len(fold), len(parts)
    whole = pl.BlockSpec(memory_space=pltpu.VMEM)
    if first:
        operands = [queries]
    else:
        operands = [state[part][0] for part in parts] + [state[part][1] for part in parts]
    operands += [array for part in parts for array, _ in kvs[part]]
    specs = [whole] * len(operands)
    aliases = {}
    if into is not None:
        specs.append(pl.BlockSpec(memory_space=pl.ANY))
        aliases = {1 + len(operands): 0}
        operands.append(into)
    extra = []
    if last:
        extra = [pltpu.VMEM((rows, half * group * HD), jnp.bfloat16), pltpu.SemaphoreType.DMA((half,))]
        out_specs = pl.BlockSpec(memory_space=pl.ANY)
        out_shape = jax.ShapeDtypeStruct((rows, width), jnp.bfloat16)
    else:
        turned = jax.ShapeDtypeStruct((half, HD, tiles_max * lanes), jnp.bfloat16)
        held = jax.ShapeDtypeStruct((half, STATE, tiles_max * lanes), jnp.float32)
        out_shape = [turned] * (many if first else 0) + [held] * many
        out_specs = [whole] * len(out_shape)
    result = pl.pallas_call(
        partial(attend, stride, moves, fold, [[block for _, block in kvs[part]] for part in parts], parts, first, last),
        grid_spec=pltpu.PrefetchScalarGridSpec(
            num_scalar_prefetch=1,
            grid=(many * steps,),
            in_specs=specs,
            out_specs=out_specs,
            scratch_shapes=[
                pltpu.VMEM((STEP, n * rows, HD), jnp.bfloat16),
                pltpu.VMEM((STEP, VROWS, n * rows), jnp.bfloat16),
                pltpu.VMEM((8, tiles_max * lanes), jnp.float32),
            ] + extra,
        ),
        out_shape=out_shape,
        input_output_aliases=aliases,
        compiler_params=pltpu.CompilerParams(vmem_limit_bytes=VMEM),
        cost_estimate=pl.CostEstimate(
            flops=2 * rows * rows * width * n * many,
            bytes_accessed=rows * width * many,
            transcendentals=rows * rows * width // HD * n // 2 * many,
        ),
        name="levels_" + str(n) + ("_first" if first else "_last" if last else ""),
    )(table, *operands)
    if last:
        return result
    state = dict(state or {})
    for at, part in enumerate(parts):
        state[part] = (result[at], result[many + at]) if first else (state[part][0], result[at])
    return state


def per_device(queries, keyvals, parent, counts):
    rows, width = queries.shape
    kv_heads = keyvals.shape[1] // (2 * HD)
    half = kv_heads // 2
    segments = lax.axis_size("tp")
    stride = segments // SPAN
    me = lax.axis_index("tp").reshape(1).astype(jnp.int32)
    table = jnp.concatenate([me, parent, counts])

    def send(x, pairs):
        full = [(a * stride + t, b * stride + t) for a, b in pairs for t in range(stride)]
        return lax.ppermute(x, "tp", full)

    def kernel(moves, kvs, state, **more):
        return levels(stride, table, queries, kv_heads, moves, kvs, state, **more)

    def halves(*arrays):
        return [[(array, part) for array in arrays] for part in (0, 1)]

    swap = [(o, o ^ 1) for o in range(SPAN)]
    up = [(o, (o + 2) % SPAN) for o in range(SPAN)]
    swap3 = [(o, o ^ 1) for o in range(4, SPAN)]
    swap4 = [(o, o ^ 1) for o in range(6, SPAN)]
    up3 = [(o, o + 2) for o in range(4, SPAN - 2)]
    cut = half * 2 * HD
    hold = lax.optimization_barrier
    m1 = [(2, False), (0, True)]
    m2 = [(4, False), (2, True)]
    m3 = [(6, False), (4, True)]
    m4 = [(6, True)]
    every = [None] + m1 + m2 + m3 + m4
    a, b = keyvals[:, :cut], keyvals[:, cut:]
    ax1, az1 = send(a, swap), send(a, up)
    bx1, bz1 = send(b, swap), send(b, up)
    state = kernel([None], [[(a, 0)], None], None, parts=(0,))
    az1, ax1, state = hold((az1, ax1, state))
    ax2 = send(az1, swap)
    az2 = send(az1, up)
    state = kernel([None], [None, [(b, 0)]], state, parts=(1,), begin=True)
    bz1, bx1, state = hold((bz1, bx1, state))
    bx2 = send(bz1, swap)
    bz2 = send(bz1, up)
    state = kernel(m1, [[(az1, 0), (ax1, 0)], [(bz1, 0), (bx1, 0)]], state, parts=(0,))
    az2, ax2, state = hold((az2, ax2, state))
    ax3 = send(az2, swap)
    az3 = send(az2, up3)
    state = kernel(m2, [[(az2, 0), (ax2, 0)], None], state, parts=(0,))
    bz2, bx2, state = hold((bz2, bx2, state))
    bx3 = send(bz2, swap)
    bz3 = send(bz2, up3)
    state = kernel(m1 + m2, [None, [(bz1, 0), (bx1, 0), (bz2, 0), (bx2, 0)]], state, parts=(1,))
    az3, ax3, state = hold((az3, ax3, state))
    a4 = send(az3, swap)
    state = kernel(m3, [[(az3, 0), (ax3, 0)], None], state, parts=(0,))
    bz3, bx3, state = hold((bz3, bx3, state))
    b4 = send(bx3, up3)
    state = kernel(m3, [None, [(bz3, 0), (bx3, 0)]], state, parts=(1,))
    of_a = [(a, 0), (az1, 0), (ax1, 0), (az2, 0), (ax2, 0), (az3, 0), (ax3, 0), (a4, 0)]
    of_b = [(b, 0), (bz1, 0), (bx1, 0), (bz2, 0), (bx2, 0), (bz3, 0), (bx3, 0), (b4, 0)]
    out = kernel(every, [of_a, None], state, parts=(0,), fold=[7], last=True)
    return kernel(every, [None, of_b], state, parts=(1,), fold=[7], last=True, into=out)

def solution(mesh):
    in_specs = (P(("rep", "tp"), None), P(("rep", "tp"), None), P("rep"), P("rep"))
    out_specs = P(("rep", "tp"), None)
    return jax.shard_map(
        per_device, mesh=mesh, in_specs=in_specs, out_specs=out_specs, check_vma=False
    )
```

```python
from functools import partial

import jax
import jax.numpy as jnp
from jax import lax
from jax.experimental import pallas as pl
from jax.experimental.pallas import tpu as pltpu
from jax.sharding import PartitionSpec as P

HD = 128
SPAN = 8
TILE = 32
NEG = -1e30
SCALE = HD ** (-0.5)
FACTOR = SCALE * 1.4426950408889634
SMALLEST, LARGEST = 2.0 ** -60, 2.0 ** 100
STATE = HD + 8
VROWS = HD + 16
TOTAL = HD
UNIT = 4
STEP = 2
VMEM = 20 * 1024 * 1024


def parent_of(table_ref, segment):
    return table_ref[1 + segment]


def count_of(table_ref, segment):
    return table_ref[1 + (table_ref.shape[0] - 1) // 2 + segment]


def is_ancestor(table_ref, me, source):
    current = me
    hit = jnp.int32(0)
    for _ in range(SPAN - 1):
        current = jnp.where(current >= 0, parent_of(table_ref, jnp.maximum(current, 0)), -1)
        hit = jnp.where(current == source, 1, hit)
    return jnp.where(source >= 0, hit, 0)


def source_of(me, stride, shift, swap):
    offset = me // stride
    base = offset
    if swap:
        base = jnp.where(offset % 2 == 0, offset + 1, offset - 1)
    base = base - shift
    return jnp.where(base >= 0, base * stride + me % stride, -1)


def live_keys(table_ref, me, stride, move):
    if move is None:
        return count_of(table_ref, me)
    source = source_of(me, stride, *move)
    length = count_of(table_ref, jnp.maximum(source, 0))
    return jnp.where(is_ancestor(table_ref, me, source) > 0, length, 0)


def attend(stride, moves, fold, blocks, parts, first, last, table_ref, *refs):
    refs = list(refs)
    many, n = len(parts), len(fold)
    if first:
        q_ref = refs.pop(0)
    else:
        qt_refs = [refs.pop(0) for _ in parts]
        old_refs = [refs.pop(0) for _ in parts]
    kv_refs = [[refs.pop(0) for _ in moves] for _ in parts]
    if last:
        if parts[0] > 0:
            refs.pop(0)
        out_ref = refs.pop(0)
    else:
        if first:
            qt_refs = [refs.pop(0) for _ in parts]
        new_refs = [refs.pop(0) for _ in parts]
    k_buf, v_buf, bad_buf = refs[:3]
    if last:
        out_buf, sems = refs[3:]

    me = table_ref[0]
    count = count_of(table_ref, me)
    held, _, across_all = qt_refs[0].shape
    rows = v_buf.shape[2] // n
    tiles_max = rows // TILE
    lanes = across_all // tiles_max
    group = lanes // TILE
    tiles = (count + TILE - 1) // TILE
    steps = held // STEP
    head = (pl.program_id(0) % steps) * STEP
    turn_of = pl.program_id(0) // steps
    lengths = {l: live_keys(table_ref, me, stride, moves[l]) for l in fold}

    def key_value(i, l, h):
        of = slice(blocks[i][l] * rows, (blocks[i][l] + 1) * rows)
        base = pl.multiple_of((head + h) * 2 * HD, 2 * HD)
        return kv_refs[i][l][of, pl.ds(base, HD)], kv_refs[i][l][of, pl.ds(base + HD, HD)]

    def fill(i):
        j = lax.broadcasted_iota(jnp.int32, (VROWS - HD, rows), 1)
        sub = lax.broadcasted_iota(jnp.int32, (VROWS - HD, rows), 0)
        for at, l in enumerate(fold):
            to = slice(at * rows, (at + 1) * rows)
            inside = jnp.where(j < lengths[l], 1.0, 0.0)
            for h in range(STEP):
                key, value = key_value(i, l, h)
                k_buf[h, to, :] = key
                v_buf[h, :HD, to] = value.T * inside[:1].astype(jnp.bfloat16)
                v_buf[h, HD:, to] = jnp.where(sub == 0, inside, 0.0).astype(jnp.bfloat16)

    def across(t, k=1):
        if isinstance(t, int):
            return slice(t * lanes, (t + k) * lanes)
        return pl.ds(pl.multiple_of(t * lanes, lanes), k * lanes)

    def down(t):
        if isinstance(t, int):
            return slice(t * TILE, (t + 1) * TILE)
        return pl.ds(pl.multiple_of(t * TILE, TILE), TILE)

    def slot(t, shape):
        lane = lax.broadcasted_iota(jnp.int32, shape, 1)
        return lane % TILE + (lane // lanes + t) * TILE

    def turned(i, h, t, k):
        if first:
            base = (parts[i] * held + head + h) * group * HD
            for u in range(k):
                heads = [
                    q_ref[down(t + u), pl.ds(pl.multiple_of(base + g * HD, HD), HD)] for g in range(group)
                ]
                qt_refs[i][head + h, :, across(t + u)] = jnp.concatenate(heads, axis=0).T
        return qt_refs[i][head + h, :, across(t, k)]

    def scores(i, h, t, k):
        return jnp.dot(k_buf[h], turned(i, h, t, k), preferred_element_type=jnp.float32)

    def write(h, t, k, mixed, total):
        live = slot(t, (1, k * lanes)) < count
        result = (mixed * jnp.where(live, 1.0 / total, 0.0)).astype(out_ref.dtype).T
        for u in range(k):
            for g in range(group):
                at = u * lanes + g * TILE
                to = pl.multiple_of((head + h) * group * HD + g * HD, HD)
                out_buf[down(t + u), pl.ds(to, HD)] = result[at:at + TILE]

    def leave(h):
        size = group * HD
        return pltpu.make_async_copy(
            out_buf.at[:, pl.ds(pl.multiple_of(h * size, size), size)],
            out_ref.at[:, pl.ds(pl.multiple_of((parts[0] * held + h) * size, size), size)],
            sems.at[h],
        )

    def unshifted(i, h, t, k, s):
        w = jnp.exp2(s * FACTOR)
        if first:
            j = lax.broadcasted_iota(jnp.int32, (rows, k * lanes), 0)
            own = jnp.where(j <= slot(t, (1, k * lanes)), w[:rows], 0.0)
            w = jnp.concatenate([own, w[rows:]], axis=0) if n > 1 else own
        mixed = jnp.dot(v_buf[h], w.astype(jnp.bfloat16), preferred_element_type=jnp.float32)[:STATE]
        if not first:
            mixed = mixed + old_refs[i][head + h, :, across(t, k)]
        if last:
            total = mixed[TOTAL:TOTAL + 1]
            good = (total >= SMALLEST) & (total <= LARGEST)
            bad_buf[pl.ds(head + h, 1), across(t, k)] = jnp.where(good, 0.0, 1.0)
            write(h, t, k, mixed[:HD], total)
        else:
            new_refs[i][head + h, :, across(t, k)] = mixed

    def settle(i, k):
        for h in range(STEP):
            mixed = old_refs[i][head + h, :, across(0, k)]
            total = mixed[TOTAL:TOTAL + 1]
            good = (total >= SMALLEST) & (total <= LARGEST)
            bad_buf[pl.ds(head + h, 1), across(0, k)] = jnp.where(good, 0.0, 1.0)
            write(h, 0, k, mixed[:HD], total)
            leave(head + h).start()

    def run(i, k):
        units = [(i, h, t, min(UNIT, k - t)) for h in range(STEP) for t in range(0, k, UNIT)]
        s = scores(*units[0])
        for at, unit in enumerate(units):
            following = scores(*units[at + 1]) if at + 1 < len(units) else None
            unshifted(*unit, s)
            if last and (at + 1 == len(units) or units[at + 1][1] != unit[1]):
                leave(head + unit[1]).start()
            s = following

    def shifted(i, h, t, _):
        q = qt_refs[i][head + h, :, across(t)]
        j = lax.broadcasted_iota(jnp.int32, (rows, lanes), 0)
        pieces = []
        for l, move in enumerate(moves):
            s = jnp.dot(key_value(i, l, h)[0], q, preferred_element_type=jnp.float32)
            allowed = j < live_keys(table_ref, me, stride, move)
            if move is None:
                allowed = allowed & (j <= slot(t, (1, lanes)))
            pieces.append(jnp.where(allowed, s, NEG))
        top = jnp.max(pieces[0], axis=0, keepdims=True)
        for s in pieces[1:]:
            top = jnp.maximum(top, jnp.max(s, axis=0, keepdims=True))
        mixed = jnp.zeros((HD, lanes), jnp.float32)
        total = jnp.zeros((1, lanes), jnp.float32)
        for l, s in enumerate(pieces):
            w = jnp.exp2((s - top) * FACTOR)
            total = total + jnp.sum(w, axis=0, keepdims=True)
            value_t = key_value(i, l, h)[1].T
            mixed = mixed + jnp.dot(value_t, w.astype(jnp.bfloat16), preferred_element_type=jnp.float32)
        write(h, t, 1, mixed, total)
        return 0

    def safely(i):
        def again(h, _):
            leave(h).wait()
            lax.fori_loop(0, tiles, partial(shifted, i, h - head), 0)
            leave(h).start()
            return 0

        lax.fori_loop(0, held, again, 0)

    def keep(i):
        for h in range(STEP):
            new_refs[i][head + h] = old_refs[i][head + h]

    if last:
        def clear(t, _):
            size = STEP * group * HD
            part = pl.ds(pl.multiple_of(head * group * HD, size), size)
            out_buf[down(t), part] = jnp.zeros((TILE, size), out_buf.dtype)
            return 0

        lax.fori_loop(tiles, tiles_max, clear, 0)

    some = sum(lengths.values()) > 0
    for i in range(many):
        here = turn_of == i if many > 1 else count > 0
        mine = here & some
        pl.when(mine)(partial(fill, i))
        if last:
            @pl.when(pl.program_id(0) == 0)
            def _():
                bad_buf[...] = jnp.zeros(bad_buf.shape, jnp.float32)

        for k in range(1, tiles_max + 1):
            pl.when(mine & (tiles == k))(partial(run, i, k))
            if last:
                pl.when(here & jnp.logical_not(some) & (tiles == k))(partial(settle, i, k))
        if last:
            @pl.when(pl.program_id(0) == steps - 1)
            def _():
                pl.when(here & (jnp.max(bad_buf[...]) > 0.0))(partial(safely, i))

        elif not first:
            pl.when(here & jnp.logical_not(some))(partial(keep, i))

    if last:
        @pl.when(pl.program_id(0) == steps - 1)
        def _():
            for h in range(held):
                leave(h).wait()


def levels(stride, table, queries, kv_heads, moves, kvs, state, parts=(0, 1), fold=None, last=False, into=None, begin=False):
    rows, width = queries.shape
    group = width // HD // kv_heads
    half = kv_heads // 2
    tiles_max = rows // TILE
    lanes = group * TILE
    first = state is None or begin
    steps = half // STEP
    fold = list(range(len(moves))) if fold is None else fold
    n, many = len(fold), len(parts)
    whole = pl.BlockSpec(memory_space=pltpu.VMEM)
    if first:
        operands = [queries]
    else:
        operands = [state[part][0] for part in parts] + [state[part][1] for part in parts]
    operands += [array for part in parts for array, _ in kvs[part]]
    specs = [whole] * len(operands)
    aliases = {}
    if into is not None:
        specs.append(pl.BlockSpec(memory_space=pl.ANY))
        aliases = {1 + len(operands): 0}
        operands.append(into)
    extra = []
    if last:
        extra = [pltpu.VMEM((rows, half * group * HD), jnp.bfloat16), pltpu.SemaphoreType.DMA((half,))]
        out_specs = pl.BlockSpec(memory_space=pl.ANY)
        out_shape = jax.ShapeDtypeStruct((rows, width), jnp.bfloat16)
    else:
        turned = jax.ShapeDtypeStruct((half, HD, tiles_max * lanes), jnp.bfloat16)
        held = jax.ShapeDtypeStruct((half, STATE, tiles_max * lanes), jnp.float32)
        out_shape = [turned] * (many if first else 0) + [held] * many
        out_specs = [whole] * len(out_shape)
    result = pl.pallas_call(
        partial(attend, stride, moves, fold, [[block for _, block in kvs[part]] for part in parts], parts, first, last),
        grid_spec=pltpu.PrefetchScalarGridSpec(
            num_scalar_prefetch=1,
            grid=(many * steps,),
            in_specs=specs,
            out_specs=out_specs,
            scratch_shapes=[
                pltpu.VMEM((STEP, n * rows, HD), jnp.bfloat16),
                pltpu.VMEM((STEP, VROWS, n * rows), jnp.bfloat16),
                pltpu.VMEM((8, tiles_max * lanes), jnp.float32),
            ] + extra,
        ),
        out_shape=out_shape,
        input_output_aliases=aliases,
        compiler_params=pltpu.CompilerParams(vmem_limit_bytes=VMEM),
        cost_estimate=pl.CostEstimate(
            flops=2 * rows * rows * width * n * many,
            bytes_accessed=rows * width * many,
            transcendentals=rows * rows * width // HD * n // 2 * many,
        ),
        name="levels_" + str(n) + ("_first" if first else "_last" if last else ""),
    )(table, *operands)
    if last:
        return result
    state = dict(state or {})
    for at, part in enumerate(parts):
        state[part] = (result[at], result[many + at]) if first else (state[part][0], result[at])
    return state


def per_device(queries, keyvals, parent, counts):
    rows, width = queries.shape
    kv_heads = keyvals.shape[1] // (2 * HD)
    half = kv_heads // 2
    segments = lax.axis_size("tp")
    stride = segments // SPAN
    me = lax.axis_index("tp").reshape(1).astype(jnp.int32)
    table = jnp.concatenate([me, parent, counts])

    def send(x, pairs):
        full = [(a * stride + t, b * stride + t) for a, b in pairs for t in range(stride)]
        return lax.ppermute(x, "tp", full)

    def kernel(moves, kvs, state, **more):
        return levels(stride, table, queries, kv_heads, moves, kvs, state, **more)

    def halves(*arrays):
        return [[(array, part) for array in arrays] for part in (0, 1)]

    swap = [(o, o ^ 1) for o in range(SPAN)]
    up = [(o, (o + 2) % SPAN) for o in range(SPAN)]
    swap3 = [(o, o ^ 1) for o in range(4, SPAN)]
    swap4 = [(o, o ^ 1) for o in range(6, SPAN)]
    up3 = [(o, o + 2) for o in range(4, SPAN - 2)]
    cut = half * 2 * HD
    hold = lax.optimization_barrier
    m1 = [(2, False), (0, True)]
    m2 = [(4, False), (2, True)]
    m3 = [(6, False), (4, True)]
    m4 = [(6, True)]
    every = [None] + m1 + m2 + m3 + m4
    a, b = keyvals[:, :cut], keyvals[:, cut:]
    ax1, az1 = send(a, swap), send(a, up)
    bx1, bz1 = send(b, swap), send(b, up)
    state = kernel([None], [[(a, 0)], None], None, parts=(0,))
    az1, ax1, state = hold((az1, ax1, state))
    ax2 = send(az1, swap)
    az2 = send(az1, up)
    state = kernel([None], [None, [(b, 0)]], state, parts=(1,), begin=True)
    bz1, bx1, state = hold((bz1, bx1, state))
    bx2 = send(bz1, swap)
    bz2 = send(bz1, up)
    state = kernel(m1, [[(az1, 0), (ax1, 0)], [(bz1, 0), (bx1, 0)]], state, parts=(0,))
    az2, ax2, state = hold((az2, ax2, state))
    ax3 = send(az2, swap)
    az3 = send(az2, up3)
    state = kernel(m2, [[(az2, 0), (ax2, 0)], None], state, parts=(0,))
    bz2, bx2, state = hold((bz2, bx2, state))
    bx3 = send(bz2, swap)
    bz3 = send(bz2, up3)
    state = kernel(m1 + m2, [None, [(bz1, 0), (bx1, 0), (bz2, 0), (bx2, 0)]], state, parts=(1,))
    az3, ax3, state = hold((az3, ax3, state))
    a4 = send(az3, swap)
    state = kernel(m3, [[(az3, 0), (ax3, 0)], None], state, parts=(0,))
    bz3, bx3, state = hold((bz3, bx3, state))
    b4 = send(bx3, up3)
    state = kernel(m3, [None, [(bz3, 0), (bx3, 0)]], state, parts=(1,))
    of_a = [(a, 0), (az1, 0), (ax1, 0), (az2, 0), (ax2, 0), (az3, 0), (ax3, 0), (a4, 0)]
    of_b = [(b, 0), (bz1, 0), (bx1, 0), (bz2, 0), (bx2, 0), (bz3, 0), (bx3, 0), (b4, 0)]
    out = kernel(every, [of_a, None], state, parts=(0,), fold=[7], last=True)
    return kernel(every, [None, of_b], state, parts=(1,), fold=[7], last=True, into=out)

def solution(mesh):
    in_specs = (P(("rep", "tp"), None), P(("rep", "tp"), None), P("rep"), P("rep"))
    out_specs = P(("rep", "tp"), None)
    return jax.shard_map(
        per_device, mesh=mesh, in_specs=in_specs, out_specs=out_specs, check_vma=False
    )
```
